32 devices in a mesh: grp: 1, ep: 16 (over z, y, x), tp: 2 (over core).
Axes of the slice: x: 2, y: 2, z: 4, core: 2. Of those that a mesh axis runs over, the one named last changes fastest.
Arguments:
- tokens: bfloat16 [1024, 3584], P(('grp', 'ep')), may hold values from -6 to 6
- scores: float32 [1024, 8], P(('grp', 'ep')), may hold values from -6 to 6
- expert_ids: int32 [1024, 8], P(('grp', 'ep')), may hold values from 0 to 15, all different within a row; in each aligned block of 64 rows (0 to 63, 64 to 127, ...) at most 64 rows name the same one
- copied: int32 [16], P('grp'), may hold values 0 or 1
- w_gate: bfloat16 [16, 3584, 1024], P('ep', None, 'tp'), may hold values from -0.09375 to 0.09375
- w_up: bfloat16 [16, 3584, 1024], P('ep', None, 'tp'), may hold values from -0.09375 to 0.09375
- w_down: bfloat16 [16, 1024, 3584], P('ep', 'tp'), may hold values from -0.1875 to 0.1875
Outputs:
- combined: bfloat16 [1024, 3584], P(('grp', 'ep'), 'tp')
The draws below stay inside these ranges and needn't reach their ends.
Inputs may be any that keep to these rules, and one draw needn't show every extreme that they name: `expert_ids`: each row names 8 different experts. Within each aligned block of 64 rows no expert is named more than 2 * 32 times, and in some block an expert is named exactly 2 * 32 times.
All inputs are finite; a program needn't handle non-finite values.
Results may differ from the reference program's by a relative error of at most 0.0065.
Values may be sent and summed in bfloat16 or wider, within the bound.
No kernel may reach another device: no remote copies, remote signals or barrier semaphores. Data moves between devices by JAX's collectives and lax.ppermute only.
A program may use at most 128 MiB of HBM per device.

```python
import math
import jax
import jax.numpy as jnp
import numpy as np
from jax import lax

D = 3584
HID = 1024
TOP = 8
TOK_DEV = 64
EXPERTS = 16
TOKENS = 1024
CAP = 32
N_EP = 16
N_TP = 2


def touch_ends(drawn, rng, low, high):
    shape = drawn.shape
    place = [jax.random.randint(jax.random.fold_in(rng, axis), (), 0, shape[axis]) for axis in range(len(shape))]
    drawn = drawn.at[tuple(place)].set(low)
    longest = shape.index(max(shape))
    place[longest] = (place[longest] + 1) % shape[longest]
    return drawn.at[tuple(place)].set(high)


def block_scale(rng, dims, cuts, least, top_value):
    level, own = 1.0, jax.random.fold_in(rng, 6)
    for axis_at, parts in cuts:
        heights = jnp.exp(jax.random.uniform(jax.random.fold_in(own, axis_at), (parts,), jnp.float32, least / len(cuts), top_value / len(cuts)))
        level = level * jnp.repeat(heights, dims[axis_at] // parts).reshape([-1 if axis == axis_at else 1 for axis in range(len(dims))])
    return level


def assign_block(rng, own, number, rows, count, top, limit, lean):
    order = jax.random.permutation(rng, count)
    heavy_load, common = shares(count, rows * top, limit, lean, True), shares(count, rows * top, limit, lean, False)
    places = jnp.arange(count)

    def named(sizes, offset_by):
        used = int((sizes > 0).sum())
        fixed = max(1, used // 4)
        shifted = fixed + (places - fixed + offset_by * (used - fixed)) % max(1, count - fixed)
        return jnp.zeros((count,), jnp.int32).at[order[jnp.where(places < fixed, places, shifted)]].set(jnp.asarray(sizes, jnp.int32))

    sizes = jnp.where(number % 4 == 0, named(heavy_load, number // 4), named(common, number - number // 4 - 1))
    mixed = jax.random.permutation(jax.random.fold_in(own, 3), count)
    giver, taker = mixed[0:count // 2 * 2:2], mixed[1:count // 2 * 2:2]
    margin = jnp.minimum(sizes[giver] - 1, limit - sizes[taker]) // 2
    margin = jnp.where((giver == order[0]) | (taker == order[0]) | (sizes[taker] == 0), 0, jnp.maximum(margin, 0))
    shifted = jax.random.randint(jax.random.fold_in(own, 4), (count // 2,), 0, 1 << 20) % (margin + 1)
    sizes = sizes.at[giver].add(-shifted).at[taker].add(shifted)
    labels = jnp.searchsorted(jnp.cumsum(sizes), jnp.arange(rows * top), side="right").astype(jnp.int32)
    listing = labels.reshape(top, rows).T
    listing = listing[jax.random.permutation(jax.random.fold_in(own, 1), rows)]
    offset_by = jax.random.randint(jax.random.fold_in(own, 2), (rows, 1), 0, top)
    return jnp.take_along_axis(listing, (jnp.arange(top)[None, :] + offset_by) % top, axis=1)


def shares(number_of, total, bound, slope, full):
    portions = [(1 << 20) // math.isqrt(standing ** slope) + 1 for standing in range(1, number_of + 1)]
    largest = bound if full else min(bound, max(-(-total // number_of), total * portions[0] // sum(portions)))
    least = 1 if total - largest >= number_of - 1 else 0
    counts, surplus = [largest] + [least] * (number_of - 1), total - largest - least * (number_of - 1)
    while surplus > 0:
        movable = [i for i in range(1, number_of) if counts[i] < largest] or [i for i in range(1, number_of) if counts[i] < bound]
        whole, budget = sum([portions[i] for i in movable]), surplus
        for i in movable:
            extra = min(bound - counts[i], max(1, budget * portions[i] // whole), surplus)
            counts[i] = counts[i] + extra
            surplus = surplus - extra
    return np.array(counts)


def bell_draw(own_key, dims, spread, bound, shards=(), kind=jnp.bfloat16):
    gain = block_scale(own_key, dims, shards, -0.22, 0.18) if shards else 1.0
    array = jax.random.normal(own_key, dims, jnp.float32) * spread * gain
    return jnp.minimum(jnp.maximum(array, -bound), bound).astype(kind)


def setup_inputs(seed: int = 0, part: int = 0) -> dict:
    streams_of = jax.random.split(jax.random.key(seed), 8)
    part_keys = jax.random.split(jax.random.fold_in(streams_of[7], part), 8)
    tokens = bell_draw(part_keys[0], (TOKENS, D), 1.0, 6.0, ((0, 16),))
    scores = bell_draw(part_keys[1], (TOKENS, TOP), 1.5, 6.0, ((0, 16),), jnp.float32)
    expert_ids_keys = jax.random.split(jax.random.fold_in(part_keys[2], 1), TOKENS // TOK_DEV)
    expert_ids_turns = jax.random.permutation(jax.random.fold_in(part_keys[2], 3), TOKENS // TOK_DEV)
    expert_ids = jax.vmap(lambda own, number: assign_block(jax.random.fold_in(part_keys[2], 2), own, number, TOK_DEV, EXPERTS, TOP, 2 * CAP, 2))(expert_ids_keys, expert_ids_turns).reshape((TOKENS, TOP))
    copied = touch_ends((jax.random.randint(part_keys[3], (EXPERTS,), 0, 4) < 3).astype(jnp.int32), jax.random.fold_in(part_keys[3], 1), 0, 1)
    w_gate = bell_draw(streams_of[4], (EXPERTS, D, HID), D ** -0.5, 0.09375, ((0, 16), (2, 2)))
    w_up = bell_draw(streams_of[5], (EXPERTS, D, HID), D ** -0.5, 0.09375, ((0, 16), (2, 2)))
    w_down = bell_draw(streams_of[6], (EXPERTS, HID, D), HID ** -0.5, 0.1875, ((0, 16), (1, 2)))
    return dict(tokens=tokens, scores=scores, expert_ids=expert_ids, copied=copied, w_gate=w_gate, w_up=w_up, w_down=w_down)


def reference(tokens, scores, expert_ids, copied, w_gate, w_up, w_down):
    pair_count = TOKENS * TOP
    affinity = jax.nn.sigmoid(scores)
    gate_weight = 2.5 * affinity / jnp.sum(affinity, axis=1, keepdims=True)
    blocked = expert_ids.reshape(N_EP, TOK_DEV * TOP)
    onehot = (blocked[:, :, None] == jnp.arange(EXPERTS, dtype=jnp.int32)[None, None, :]).astype(jnp.int32)
    earlier = jnp.cumsum(onehot, axis=1) - onehot
    row_rank = jnp.sum(earlier * onehot, axis=2).reshape(pair_count).astype(jnp.int32)
    flat_ids = expert_ids.reshape(pair_count)
    flagged = copied[flat_ids]
    is_kept = (row_rank < CAP) | (flagged == 1)
    block_index = jnp.arange(pair_count, dtype=jnp.int32) // (TOK_DEV * TOP)
    slot_count = N_EP * 2 * CAP
    position = jnp.where(is_kept, flat_ids * slot_count + block_index * (2 * CAP) + row_rank, EXPERTS * slot_count).astype(jnp.int32)
    token_of = jnp.arange(pair_count, dtype=jnp.int32) // TOP
    row_table = jnp.full((EXPERTS * slot_count,), TOKENS, jnp.int32).at[position].set(token_of, mode="drop")
    padded = jnp.concatenate([tokens, jnp.zeros((1, D), tokens.dtype)], axis=0)
    part_width = HID // N_TP

    def expert_rows(expert):
        picks = lax.dynamic_slice_in_dim(row_table, expert * slot_count, slot_count)
        row_block = padded[picks]
        gate_act = jnp.dot(row_block, w_gate[expert], preferred_element_type=jnp.float32)
        up_act = jnp.dot(row_block, w_up[expert], preferred_element_type=jnp.float32)
        hidden = (jax.nn.silu(gate_act) * up_act).astype(jnp.bfloat16)
        total = jnp.zeros((slot_count, D), jnp.float32)
        for part in range(N_TP):
            lower = part * part_width
            product = jnp.dot(hidden[:, lower:lower + part_width], w_down[expert, lower:lower + part_width, :], preferred_element_type=jnp.float32)
            rounded = lax.optimization_barrier(product.astype(jnp.bfloat16))
            total = total + rounded.astype(jnp.float32)
        return total.astype(jnp.bfloat16)

    expert_out = lax.map(expert_rows, jnp.arange(EXPERTS, dtype=jnp.int32))
    flat_out = jnp.concatenate([expert_out.reshape(EXPERTS * slot_count, D), jnp.zeros((1, D), jnp.bfloat16)], axis=0)
    picked = flat_out[jnp.minimum(position, EXPERTS * slot_count)]
    weight = jnp.where(is_kept, gate_weight.reshape(pair_count), jnp.float32(0.0))
    terms = picked.astype(jnp.float32) * weight[:, None]
    combined = jnp.sum(terms.reshape(TOKENS, TOP, D), axis=1)
    return combined.astype(jnp.bfloat16)
```

```python
import jax
import jax.numpy as jnp
from jax import lax
from jax.sharding import PartitionSpec as P

BF16 = jnp.bfloat16
F32 = jnp.float32
QUAD = 4


def route_weights(scores, expert_ids, copied, experts, capacity):
    rows = scores.shape[0]
    affinity = jax.nn.sigmoid(scores)
    gate_weight = 2.5 * affinity / jnp.sum(affinity, axis=1, keepdims=True)
    chosen = expert_ids[:, :, None] == jnp.arange(experts, dtype=jnp.int32)[None, None, :]
    member = jnp.any(chosen, axis=1)
    weight = jnp.sum(jnp.where(chosen, gate_weight[:, :, None], 0.0), axis=1)
    at = jnp.arange(rows, dtype=jnp.int32)
    below = (at[:, None] > at[None, :]).astype(BF16)
    rank = jnp.dot(below, member.astype(BF16), preferred_element_type=F32)
    kept = (rank < capacity) | (copied[None, :] == 1)
    return jnp.where(kept, weight, 0.0)


def body(tokens, scores, expert_ids, copied, w_gate, w_up, w_down):
    ep = lax.axis_size("ep")
    me = lax.axis_index("ep")
    core = lax.axis_index("tp")
    rows, width = tokens.shape
    top = expert_ids.shape[1]
    planes = ep // QUAD
    half = rows // 2
    share = width // 2
    capacity = min(rows * top // ep, rows // 2)

    def first_link(a):
        pairs = [(2 * e + c, 2 * (e ^ (1 + c)) + c) for e in range(ep) for c in range(2)]
        return lax.ppermute(a, ("ep", "tp"), pairs)

    def second_link(a):
        pairs = [(2 * e + c, 2 * (e ^ (2 - c)) + c) for e in range(ep) for c in range(2)]
        return lax.ppermute(a, ("ep", "tp"), pairs)

    def ring(a):
        return lax.ppermute(a, "ep", [(e, (e + QUAD) % ep) for e in range(ep)])

    def other_core(a):
        return lax.ppermute(a, "tp", [(0, 1), (1, 0)])

    down_mine = lax.dynamic_slice_in_dim(w_down[0], core * share, share, 1)
    down_sent = lax.dynamic_slice_in_dim(w_down[0], (1 - core) * share, share, 1)
    down = jnp.concatenate([down_mine, other_core(down_sent)], axis=0)

    weight = route_weights(scores, expert_ids, copied, ep, capacity)
    high = weight.astype(BF16)
    low = (weight - high.astype(F32)).astype(BF16)
    pad = -(2 * ep) % 128
    wide = jnp.concatenate([tokens, high, low, jnp.zeros((rows, pad), BF16)], axis=1)
    block = lax.dynamic_slice_in_dim(wide, core * half, half, 0)

    lane = jnp.arange(2 * ep + pad, dtype=jnp.int32)
    mine = ((lane == me) | (lane == me + ep)).astype(F32)

    def gather(block):
        pair = jnp.concatenate([block, first_link(block)], axis=0)
        far = second_link(pair)
        held = jnp.concatenate([pair, far], axis=0)
        theirs = other_core(held)
        m = held.reshape(QUAD, half, -1)
        o = theirs.reshape(QUAD, half, -1)
        kept = jnp.concatenate([m[0], m[2], o[0], o[1]], axis=0)
        sent = jnp.concatenate([m[1], m[3], o[2], o[3]], axis=0)
        return jnp.concatenate([kept, sent], axis=0)

    def experts(x):
        flat = x[:, :width]
        gate = jnp.dot(flat, w_gate[0], preferred_element_type=F32)
        up = jnp.dot(flat, w_up[0], preferred_element_type=F32)
        hidden = (jax.nn.silu(gate) * up).astype(BF16)
        r = other_core(hidden).reshape(2 * QUAD, half, -1)
        swapped = jnp.concatenate([r[2], r[6], r[0], r[4], r[3], r[7], r[1], r[5]], axis=0)
        both = jnp.concatenate([hidden, swapped], axis=1)
        scale = jnp.sum(x[:, width:].astype(F32) * mine[None, :], axis=1, keepdims=True)
        return jnp.dot(both, down, preferred_element_type=F32) * scale

    def scatter(y):
        n = y.shape[0] // 2
        got = first_link(y[n:].astype(BF16))
        part = (y[:n] + got.astype(F32)).reshape(2, 2, half, share)
        far = second_link(part[:, 1].reshape(2 * half, share).astype(BF16))
        return part[:, 0].reshape(2 * half, share) + far.astype(F32)

    blocks = [block]
    for _ in range(planes - 1):
        blocks.append(ring(blocks[-1]))
    outs = [experts(gather(b)) for b in blocks]
    total = None
    for step in list(range(1, planes)) + [0]:
        part = scatter(outs[step])
        total = part if total is None else ring(total.astype(BF16)).astype(F32) + part
    mine_rows, other_rows = total[:half], total[half:]
    first = jnp.where(core == 0, mine_rows, other_rows)
    second = jnp.where(core == 0, other_rows, mine_rows)
    return jnp.concatenate([first, second], axis=0).astype(BF16)


def solution(mesh):
    in_specs = (
        P(("grp", "ep"), None),
        P(("grp", "ep"), None),
        P(("grp", "ep"), None),
        P("grp"),
        P("ep", None, "tp"),
        P("ep", None, "tp"),
        P("ep", "tp", None),
    )
    out_specs = P(("grp", "ep"), "tp")
    return jax.shard_map(body, mesh=mesh, in_specs=in_specs, out_specs=out_specs, check_vma=False)
```

```python
import functools

import jax
import jax.numpy as jnp
from jax import lax
from jax.experimental import pallas as pl
from jax.experimental.pallas import tpu as pltpu
from jax.sharding import PartitionSpec as P

BF16 = jnp.bfloat16
F32 = jnp.float32
QUAD = 4
LANES = 128
VMEM = pltpu.VMEM


def route_kernel(experts, capacity, aside, core_ref, copied_ref, tokens_ref, scores_ref, ids_ref, block_ref):
    rows, top = scores_ref.shape
    half, width = tokens_ref.shape
    affinity = 1.0 / (1.0 + jnp.exp(-scores_ref[...]))
    gate = 2.5 * affinity / jnp.sum(affinity, axis=1, keepdims=True)
    ids = ids_ref[...]
    lane = lax.broadcasted_iota(jnp.int32, (rows, aside), 1)
    expert = jnp.where(lane < experts, lane, jnp.where(lane < 2 * experts, lane - experts, -1))
    member = jnp.zeros((rows, aside), F32)
    weight = jnp.zeros((rows, aside), F32)
    for k in range(top):
        here = ids[:, k : k + 1] == expert
        member = jnp.where(here, 1.0, member)
        weight = jnp.where(here, gate[:, k : k + 1], weight)
    copied = jnp.zeros((1, aside), jnp.int32)
    for e in range(experts):
        copied = jnp.where(expert[:1] == e, copied_ref[e], copied)
    below = lax.broadcasted_iota(jnp.int32, (rows, rows), 0) > lax.broadcasted_iota(jnp.int32, (rows, rows), 1)
    rank = jnp.dot(below.astype(F32).astype(BF16), member.astype(BF16), preferred_element_type=F32)
    kept = (rank < capacity) | (copied == 1)
    weight = jnp.where(kept, weight, 0.0)
    weight = jnp.where(core_ref[0] == 0, weight[:half], weight[half:])
    high = weight.astype(BF16).astype(F32)
    block_ref[:, :width] = tokens_ref[...]
    block_ref[:, width:] = jnp.where(lane[:half] < experts, high, weight - high).astype(BF16)


def hidden_kernel(experts, me_ref, *refs):
    pieces, (gate_ref, up_ref, hidden_ref, scale_ref) = refs[:4], refs[4:]
    width, units = gate_ref.shape
    n = pieces[0].shape[0]
    x = jnp.concatenate([p[:, :width] for p in pieces], axis=0)
    step = 256 if units % 256 == 0 else units
    for at in range(0, units, step):
        gate = jnp.dot(x, gate_ref[:, at : at + step], preferred_element_type=F32)
        up = jnp.dot(x, up_ref[:, at : at + step], preferred_element_type=F32)
        hidden_ref[:, at : at + step] = (gate / (1.0 + jnp.exp(-gate)) * up).astype(BF16)
    for i, p in enumerate(pieces):
        beside = p[:, width:].astype(F32)
        lane = lax.broadcasted_iota(jnp.int32, beside.shape, 1)
        mine = (lane == me_ref[0]) | (lane == me_ref[0] + experts)
        total = jnp.sum(jnp.where(mine, beside, 0.0), axis=1, keepdims=True)
        scale_ref[i * n : (i + 1) * n, :] = jnp.broadcast_to(total, (n, LANES))


def down_kernel(half, hidden_ref, other_ref, scale_ref, mine_ref, received_ref, kept_ref, sent_ref):
    n = hidden_ref.shape[0] // 2
    share = mine_ref.shape[1]
    hidden = hidden_ref[...]
    other = jnp.concatenate([other_ref[n:, :], other_ref[:n, :]], axis=0)
    scale = scale_ref[:, :1]
    step = 256 if share % 256 == 0 else share
    for at in range(0, share, step):
        y = jnp.dot(hidden, mine_ref[:, at : at + step], preferred_element_type=F32)
        y = y + jnp.dot(other, received_ref[:, at : at + step], preferred_element_type=F32)
        y = y * scale
        for ref, order in ((kept_ref, (0, 2, 4, 5)), (sent_ref, (1, 3, 6, 7))):
            for i, j in enumerate(order):
                ref[i * half : (i + 1) * half, at : at + step] = y[j * half : (j + 1) * half].astype(ref.dtype)


def call(kernel, outs, args, scalars=0, flops=0):
    spaces = [pltpu.SMEM] * scalars + [VMEM] * (len(args) - scalars)
    return pl.pallas_call(
        kernel,
        out_shape=outs,
        in_specs=[pl.BlockSpec(memory_space=s) for s in spaces],
        out_specs=jax.tree.map(lambda _: pl.BlockSpec(memory_space=VMEM), outs),
        compiler_params=pltpu.CompilerParams(vmem_limit_bytes=32 << 20),
        cost_estimate=pl.CostEstimate(flops=flops, bytes_accessed=sum(a.size * a.dtype.itemsize for a in args), transcendentals=0),
    )(*args)


def after(a, *deps):
    return lax.optimization_barrier((a,) + deps)[0]


def body(tokens, scores, expert_ids, copied, w_gate, w_up, w_down):
    ep = lax.axis_size("ep")
    me = lax.axis_index("ep").astype(jnp.int32)[None]
    core = lax.axis_index("tp")
    rows, width = tokens.shape
    top = expert_ids.shape[1]
    units = w_gate.shape[2]
    planes = ep // QUAD
    half = rows // 2
    share = width // 2
    quad_rows = QUAD * rows
    capacity = min(rows * top // ep, rows // 2)
    aside = -(-2 * ep // LANES) * LANES

    def first_link(a):
        pairs = [(2 * e + c, 2 * (e ^ (1 + c)) + c) for e in range(ep) for c in range(2)]
        return lax.ppermute(a, ("ep", "tp"), pairs)

    def second_link(a):
        pairs = [(2 * e + c, 2 * (e ^ (2 - c)) + c) for e in range(ep) for c in range(2)]
        return lax.ppermute(a, ("ep", "tp"), pairs)

    def ring(a):
        return lax.ppermute(a, "ep", [(e, (e + QUAD) % ep) for e in range(ep)])

    def other_core(a):
        return lax.ppermute(a, "tp", [(0, 1), (1, 0)])

    block = pl.pallas_call(
        functools.partial(route_kernel, ep, capacity, aside),
        out_shape=jax.ShapeDtypeStruct((half, width + aside), BF16),
        grid_spec=pltpu.PrefetchScalarGridSpec(
            num_scalar_prefetch=1,
            grid=(1,),
            in_specs=[
                pl.BlockSpec(memory_space=pltpu.SMEM),
                pl.BlockSpec((half, width), lambda i, c: (c[0], 0)),
                pl.BlockSpec((rows, top), lambda i, c: (0, 0)),
                pl.BlockSpec((rows, top), lambda i, c: (0, 0)),
            ],
            out_specs=pl.BlockSpec((half, width + aside), lambda i, c: (0, 0)),
        ),
    )(core.astype(jnp.int32)[None], copied, tokens, scores, expert_ids)

    def experts(pair, far, tpair, tfar):
        hidden, scale = call(
            functools.partial(hidden_kernel, ep),
            (
                jax.ShapeDtypeStruct((quad_rows, units), BF16),
                jax.ShapeDtypeStruct((quad_rows, LANES), F32),
            ),
            (me, pair, far, tpair, tfar, w_gate[0], w_up[0]),
            scalars=1,
            flops=4 * quad_rows * width * units,
        )
        return hidden, scale, other_core(hidden)

    def finish(hidden, scale, other):
        return call(
            functools.partial(down_kernel, half),
            (
                jax.ShapeDtypeStruct((quad_rows // 2, share), F32),
                jax.ShapeDtypeStruct((quad_rows // 2, share), BF16),
            ),
            (hidden, other, scale, down_mine, down_received),
            flops=4 * quad_rows * share * units,
        )

    def scatter(kept, sent):
        got = first_link(sent)
        part = (kept + got.astype(F32)).reshape(2, 2, half, share)
        far = second_link(part[:, 1].reshape(2 * half, share).astype(BF16))
        return part[:, 0].reshape(2 * half, share) + far.astype(F32)

    blocks = [block]
    near = [first_link(block)]
    for _ in range(planes - 1):
        blocks.append(ring(blocks[-1]))
        near.append(None)
    w_down_later = after(w_down[0], near[0])
    down_mine = lax.dynamic_slice_in_dim(w_down_later, core * share, share, 1)
    down_received = other_core(lax.dynamic_slice_in_dim(w_down_later, (1 - core) * share, share, 1))

    outs = []
    for s in range(planes):
        pair = jnp.concatenate([blocks[s], near[s]], axis=0)
        far = second_link(pair)
        if s + 1 < planes:
            nxt = blocks[s + 1]
            if s >= 1:
                nxt = after(nxt, outs[s - 1][1])
            near[s + 1] = first_link(nxt)
        outs.append(finish(*experts(pair, far, other_core(pair), other_core(far))))
    total = None
    for s in list(range(1, planes)) + [0]:
        part = scatter(*outs[s])
        total = part if total is None else ring(total.astype(BF16)).astype(F32) + part
    mine_rows, other_rows = total[:half], total[half:]
    first = jnp.where(core == 0, mine_rows, other_rows)
    second = jnp.where(core == 0, other_rows, mine_rows)
    return jnp.concatenate([first, second], axis=0).astype(BF16)


def solution(mesh):
    in_specs = (
        P(("grp", "ep"), None),
        P(("grp", "ep"), None),
        P(("grp", "ep"), None),
        P("grp"),
        P("ep", None, "tp"),
        P("ep", None, "tp"),
        P("ep", "tp", None),
    )
    out_specs = P(("grp", "ep"), "tp")
    return jax.shard_map(body, mesh=mesh, in_specs=in_specs, out_specs=out_specs, check_vma=False)
```

```python
import functools

import jax
import jax.numpy as jnp
from jax import lax
from jax.experimental import pallas as pl
from jax.experimental.pallas import tpu as pltpu
from jax.sharding import PartitionSpec as P

BF16 = jnp.bfloat16
F32 = jnp.float32
QUAD = 4
LANES = 128
VMEM = pltpu.VMEM


def route_kernel(experts, capacity, aside, tokens_ref, copied_ref, scores_ref, ids_ref, block_ref, sem):
    top, rows = scores_ref.shape
    half, width = rows // 2, tokens_ref.shape[1]
    core = lax.axis_index("tp")
    copy = pltpu.make_async_copy(
        tokens_ref.at[pl.ds(pl.multiple_of(core * half, half), half), :], block_ref.at[:, :width], sem
    )
    copy.start()
    affinity = 1.0 / (1.0 + jnp.exp(-scores_ref[...]))
    gate = 2.5 * affinity / jnp.sum(affinity, axis=0, keepdims=True)
    ids = ids_ref[...]
    lane = lax.broadcasted_iota(jnp.int32, (aside, rows), 0)
    expert = jnp.where(lane < experts, lane, jnp.where(lane < 2 * experts, lane - experts, -1))
    member = jnp.zeros((aside, rows), F32)
    weight = jnp.zeros((aside, rows), F32)
    for k in range(top):
        here = ids[k : k + 1, :] == expert
        member = jnp.where(here, 1.0, member)
        weight = jnp.where(here, gate[k : k + 1, :], weight)
    copied = jnp.zeros((aside, 1), jnp.int32)
    for e in range(experts):
        copied = jnp.where(expert[:, :1] == e, copied_ref[e], copied)
    above = lax.broadcasted_iota(jnp.int32, (rows, rows), 0) < lax.broadcasted_iota(jnp.int32, (rows, rows), 1)
    rank = jnp.dot(member.astype(BF16), above.astype(F32).astype(BF16), preferred_element_type=F32)
    kept = (rank < capacity) | (copied == 1)
    weight = jnp.where(kept, weight, 0.0)
    high = weight.astype(BF16).astype(F32)
    beside = jnp.where(lane < experts, high, weight - high).T
    beside = jnp.where(core == 0, beside[:half], beside[half:])
    block_ref[:, width:] = beside.astype(BF16)
    copy.wait()


def load_kernel(gate_hbm, up_hbm, down_hbm, gate_ref, up_ref, mine_ref, sent_ref, sems):
    share = mine_ref.shape[1]
    core = lax.axis_index("tp")
    here = pl.multiple_of(core * share, LANES)
    there = pl.multiple_of((1 - core) * share, LANES)
    copies = [
        pltpu.make_async_copy(down_hbm.at[0, :, pl.ds(there, share)], sent_ref, sems.at[0]),
        pltpu.make_async_copy(gate_hbm.at[0], gate_ref, sems.at[1]),
        pltpu.make_async_copy(up_hbm.at[0], up_ref, sems.at[2]),
        pltpu.make_async_copy(down_hbm.at[0, :, pl.ds(here, share)], mine_ref, sems.at[3]),
    ]
    for c in copies:
        c.start()
    for c in copies:
        c.wait()


def hidden_kernel(experts, *refs):
    pieces, (gate_ref, up_ref, hidden_ref, scale_ref) = refs[:4], refs[4:]
    width, units = gate_ref.shape
    me = lax.axis_index("ep")
    n = pieces[0].shape[0]
    x = jnp.concatenate([p[:, :width] for p in pieces], axis=0)
    step = 256 if units % 256 == 0 else units
    for at in range(0, units, step):
        gate = jnp.dot(x, gate_ref[:, at : at + step], preferred_element_type=F32)
        up = jnp.dot(x, up_ref[:, at : at + step], preferred_element_type=F32)
        hidden_ref[:, at : at + step] = (gate / (1.0 + jnp.exp(-gate)) * up).astype(BF16)
    for i, p in enumerate(pieces):
        beside = p[:, width:].astype(F32)
        lane = lax.broadcasted_iota(jnp.int32, beside.shape, 1)
        mine = (lane == me) | (lane == me + experts)
        total = jnp.sum(jnp.where(mine, beside, 0.0), axis=1, keepdims=True)
        scale_ref[i * n : (i + 1) * n, :] = jnp.broadcast_to(total, (n, LANES))


def down_kernel(half, hidden_ref, other_ref, scale_ref, mine_ref, received_ref, kept_ref, sent_ref):
    n = hidden_ref.shape[0] // 2
    share = mine_ref.shape[1]
    hidden = hidden_ref[...]
    other = jnp.concatenate([other_ref[n:, :], other_ref[:n, :]], axis=0)
    scale = scale_ref[:, :1]
    step = 256 if share % 256 == 0 else share
    for at in range(0, share, step):
        y = jnp.dot(hidden, mine_ref[:, at : at + step], preferred_element_type=F32)
        y = y + jnp.dot(other, received_ref[:, at : at + step], preferred_element_type=F32)
        y = y * scale
        for ref, order in ((kept_ref, (0, 2, 4, 5)), (sent_ref, (1, 3, 6, 7))):
            for i, j in enumerate(order):
                ref[i * half : (i + 1) * half, at : at + step] = y[j * half : (j + 1) * half].astype(ref.dtype)


def call(kernel, outs, args, spaces=None, scratch=(), flops=0, limit=32 << 20):
    spaces = spaces or [VMEM] * len(args)
    return pl.pallas_call(
        kernel,
        out_shape=outs,
        in_specs=[pl.BlockSpec(memory_space=s) for s in spaces],
        out_specs=jax.tree.map(lambda _: pl.BlockSpec(memory_space=VMEM), outs),
        scratch_shapes=scratch,
        compiler_params=pltpu.CompilerParams(vmem_limit_bytes=limit),
        cost_estimate=pl.CostEstimate(flops=flops, bytes_accessed=sum(a.size * a.dtype.itemsize for a in args), transcendentals=0),
    )(*args)


def after(a, *deps):
    return lax.optimization_barrier((a,) + deps)[0]


def body(tokens, scores, expert_ids, copied, w_gate, w_up, w_down):
    ep = lax.axis_size("ep")
    core = lax.axis_index("tp")
    rows, width = tokens.shape
    top = expert_ids.shape[1]
    units = w_gate.shape[2]
    planes = ep // QUAD
    half = rows // 2
    share = width // 2
    quad_rows = QUAD * rows
    capacity = min(rows * top // ep, rows // 2)
    aside = -(-2 * ep // LANES) * LANES

    def first_link(a):
        pairs = [(2 * e + c, 2 * (e ^ (1 + c)) + c) for e in range(ep) for c in range(2)]
        return lax.ppermute(a, ("ep", "tp"), pairs)

    def second_link(a):
        pairs = [(2 * e + c, 2 * (e ^ (2 - c)) + c) for e in range(ep) for c in range(2)]
        return lax.ppermute(a, ("ep", "tp"), pairs)

    def ring(a):
        return lax.ppermute(a, "ep", [(e, (e + QUAD) % ep) for e in range(ep)])

    def other_core(a):
        return lax.ppermute(a, "tp", [(0, 1), (1, 0)])

    block = call(
        functools.partial(route_kernel, ep, capacity, aside),
        jax.ShapeDtypeStruct((half, width + aside), BF16),
        (tokens, copied, scores.T, expert_ids.T),
        spaces=[pl.ANY, pltpu.SMEM, VMEM, VMEM],
        scratch=[pltpu.SemaphoreType.DMA],
        limit=None,
    )

    def load(gate, up, down):
        return call(
            load_kernel,
            (
                jax.ShapeDtypeStruct((width, units), BF16),
                jax.ShapeDtypeStruct((width, units), BF16),
                jax.ShapeDtypeStruct((units, share), BF16),
                jax.ShapeDtypeStruct((units, share), BF16),
            ),
            (gate, up, down),
            spaces=[pl.ANY] * 3,
            scratch=[pltpu.SemaphoreType.DMA((4,))],
            limit=41 << 20,
        )

    def experts(pair, far, tpair, tfar):
        hidden, scale = call(
            functools.partial(hidden_kernel, ep),
            (
                jax.ShapeDtypeStruct((quad_rows, units), BF16),
                jax.ShapeDtypeStruct((quad_rows, LANES), F32),
            ),
            (pair, far, tpair, tfar, gate, up),
            flops=4 * quad_rows * width * units,
        )
        return hidden, scale, other_core(hidden)

    def finish(hidden, scale, other):
        return call(
            functools.partial(down_kernel, half),
            (
                jax.ShapeDtypeStruct((quad_rows // 2, share), F32),
                jax.ShapeDtypeStruct((quad_rows // 2, share), BF16),
            ),
            (hidden, other, scale, down_mine, down_received),
            flops=4 * quad_rows * share * units,
        )

    def join(a, b):
        return jnp.concatenate([a, b], axis=0)

    def add_up(p, *ties):
        part = after(sums[p][0], *ties) + gots[p].astype(F32)
        part = part.reshape(2, 2, half, share)
        passes[p] = part[:, 1].reshape(2 * half, share).astype(BF16)
        parts[p] = part[:, 0].reshape(2 * half, share), second_link(passes[p])

    coming = ring(block)
    near = first_link(block)
    gate, up, down_mine, down_sent = load(*lax.optimization_barrier((w_gate, w_up, w_down, block))[:3])
    down_received = other_core(down_sent)
    blocks, pairs, fars = [block, coming], {}, {}
    held, sums, gots, parts, passes = {}, {}, {}, {}, {}
    marks = [down_mine]
    for i in range(planes + 2):
        if i < planes:
            if 1 <= i < planes - 1:
                blocks.append(coming)
                marks.append(coming)
            pairs[i] = join(after(blocks[i], *marks), near)
            fars[i] = second_link(pairs[i])
            marks = [fars[i]]
            if i + 1 < planes:
                if i == 0:
                    blocks[1] = after(coming, pairs[0])
                if i + 2 < planes:
                    coming = ring(blocks[i + 1])
                near = first_link(blocks[i + 1])
        p = i - 1
        if 0 <= p < planes:
            ties = [pairs[i]] if i < planes else []
            ties += [sums[p - 1][1]] if p - 1 in sums else []
            far = after(fars[p], *ties) if ties else fars[p]
            held[p] = experts(pairs[p], far, other_core(pairs[p]), other_core(far))
            marks.append(held[p][0])
        p = i - 2
        if 1 <= p < planes:
            ties = [pairs[i]] if i in pairs else []
            sums[p] = finish(after(held[p][0], *ties) if ties else held[p][0], *held[p][1:])
            gots[p] = first_link(sums[p][1])
            if p > 1:
                add_up(p - 1, sums[p][1])
    add_up(planes - 1)
    sums[0] = finish(after(held[0][0], passes[planes - 1]), *held[0][1:])
    gots[0] = first_link(sums[0][1])
    carried = None
    for p in range(1, planes):
        total = parts[p][0] + parts[p][1].astype(F32)
        passing = (total if carried is None else carried.astype(F32) + total).astype(BF16)
        carried = ring(passing)
    add_up(0, passing)
    total = carried.astype(F32) + parts[0][0] + parts[0][1].astype(F32)
    mine_rows, other_rows = total[:half], total[half:]
    first = jnp.where(core == 0, mine_rows, other_rows)
    second = jnp.where(core == 0, other_rows, mine_rows)
    return jnp.concatenate([first, second], axis=0).astype(BF16)


def solution(mesh):
    in_specs = (
        P(("grp", "ep"), None),
        P(("grp", "ep"), None),
        P(("grp", "ep"), None),
        P("grp"),
        P("ep", None, "tp"),
        P("ep", None, "tp"),
        P("ep", "tp", None),
    )
    out_specs = P(("grp", "ep"), "tp")
    return jax.shard_map(body, mesh=mesh, in_specs=in_specs, out_specs=out_specs, check_vma=False)
```

```python
import functools

import jax
import jax.numpy as jnp
from jax import lax
from jax.experimental import pallas as pl
from jax.experimental.pallas import tpu as pltpu
from jax.sharding import PartitionSpec as P

BF16 = jnp.bfloat16
F32 = jnp.float32
QUAD = 4
LANES = 128
VMEM = pltpu.VMEM


def route_kernel(experts, capacity, aside, tokens_ref, copied_ref, scores_ref, ids_ref, block_ref, sem):
    top, rows = scores_ref.shape
    half, width = rows // 2, tokens_ref.shape[1]
    core = lax.axis_index("tp")
    copy = pltpu.make_async_copy(
        tokens_ref.at[pl.ds(pl.multiple_of(core * half, half), half), :], block_ref.at[:, :width], sem
    )
    copy.start()
    affinity = 1.0 / (1.0 + jnp.exp(-scores_ref[...]))
    gate = 2.5 * affinity / jnp.sum(affinity, axis=0, keepdims=True)
    ids = ids_ref[...]
    lane = lax.broadcasted_iota(jnp.int32, (aside, rows), 0)
    expert = jnp.where(lane < experts, lane, jnp.where(lane < 2 * experts, lane - experts, -1))
    member = jnp.zeros((aside, rows), F32)
    weight = jnp.zeros((aside, rows), F32)
    for k in range(top):
        here = ids[k : k + 1, :] == expert
        member = jnp.where(here, 1.0, member)
        weight = jnp.where(here, gate[k : k + 1, :], weight)
    copied = jnp.zeros((aside, 1), jnp.int32)
    for e in range(experts):
        copied = jnp.where(expert[:, :1] == e, copied_ref[e], copied)
    above = lax.broadcasted_iota(jnp.int32, (rows, rows), 0) < lax.broadcasted_iota(jnp.int32, (rows, rows), 1)
    rank = jnp.dot(member.astype(BF16), above.astype(F32).astype(BF16), preferred_element_type=F32)
    kept = (rank < capacity) | (copied == 1)
    weight = jnp.where(kept, weight, 0.0)
    high = weight.astype(BF16).astype(F32)
    beside = jnp.where(lane < experts, high, weight - high).T
    beside = jnp.where(core == 0, beside[:half], beside[half:])
    block_ref[:, width:] = beside.astype(BF16)
    copy.wait()


def load_kernel(gate_hbm, up_hbm, down_hbm, gate_ref, up_ref, mine_ref, sent_ref, sems):
    share = mine_ref.shape[1]
    core = lax.axis_index("tp")
    here = pl.multiple_of(core * share, LANES)
    there = pl.multiple_of((1 - core) * share, LANES)
    copies = [
        pltpu.make_async_copy(down_hbm.at[0, :, pl.ds(there, share)], sent_ref, sems.at[0]),
        pltpu.make_async_copy(gate_hbm.at[0], gate_ref, sems.at[1]),
        pltpu.make_async_copy(up_hbm.at[0], up_ref, sems.at[2]),
        pltpu.make_async_copy(down_hbm.at[0, :, pl.ds(here, share)], mine_ref, sems.at[3]),
    ]
    for c in copies:
        c.start()
    for c in copies:
        c.wait()


def hidden_kernel(experts, *refs):
    pieces, (gate_ref, up_ref, hidden_ref, scale_ref) = refs[:4], refs[4:]
    width, units = gate_ref.shape
    me = lax.axis_index("ep")
    n = pieces[0].shape[0]
    x = jnp.concatenate([p[:, :width] for p in pieces], axis=0)
    step = 256 if units % 256 == 0 else units
    for at in range(0, units, step):
        gate = jnp.dot(x, gate_ref[:, at : at + step], preferred_element_type=F32)
        up = jnp.dot(x, up_ref[:, at : at + step], preferred_element_type=F32)
        hidden_ref[:, at : at + step] = (gate / (1.0 + jnp.exp(-gate)) * up).astype(BF16)
    for i, p in enumerate(pieces):
        beside = p[:, width:].astype(F32)
        lane = lax.broadcasted_iota(jnp.int32, beside.shape, 1)
        mine = (lane == me) | (lane == me + experts)
        total = jnp.sum(jnp.where(mine, beside, 0.0), axis=1, keepdims=True)
        scale_ref[i * n : (i + 1) * n, :] = jnp.broadcast_to(total, (n, LANES))


def down_kernel(half, hidden_ref, other_ref, scale_ref, mine_ref, received_ref, kept_ref, sent_ref):
    n = hidden_ref.shape[0] // 2
    share = mine_ref.shape[1]
    hidden = hidden_ref[...]
    other = jnp.concatenate([other_ref[n:, :], other_ref[:n, :]], axis=0)
    scale = scale_ref[:, :1]
    step = 256 if share % 256 == 0 else share
    for at in range(0, share, step):
        y = jnp.dot(hidden, mine_ref[:, at : at + step], preferred_element_type=F32)
        y = y + jnp.dot(other, received_ref[:, at : at + step], preferred_element_type=F32)
        y = y * scale
        for ref, order in ((kept_ref, (0, 2, 4, 5)), (sent_ref, (1, 3, 6, 7))):
            for i, j in enumerate(order):
                ref[i * half : (i + 1) * half, at : at + step] = y[j * half : (j + 1) * half].astype(ref.dtype)


def call(kernel, outs, args, spaces=None, scratch=(), flops=0, limit=32 << 20):
    spaces = spaces or [VMEM] * len(args)
    return pl.pallas_call(
        kernel,
        out_shape=outs,
        in_specs=[pl.BlockSpec(memory_space=s) for s in spaces],
        out_specs=jax.tree.map(lambda _: pl.BlockSpec(memory_space=VMEM), outs),
        scratch_shapes=scratch,
        compiler_params=pltpu.CompilerParams(vmem_limit_bytes=limit),
        cost_estimate=pl.CostEstimate(flops=flops, bytes_accessed=sum(a.size * a.dtype.itemsize for a in args), transcendentals=0),
    )(*args)


def after(a, *deps):
    return lax.optimization_barrier((a,) + deps)[0]


def body(tokens, scores, expert_ids, copied, w_gate, w_up, w_down):
    ep = lax.axis_size("ep")
    core = lax.axis_index("tp")
    rows, width = tokens.shape
    top = expert_ids.shape[1]
    units = w_gate.shape[2]
    planes = ep // QUAD
    half = rows // 2
    share = width // 2
    quad_rows = QUAD * rows
    capacity = min(rows * top // ep, rows // 2)
    aside = -(-2 * ep // LANES) * LANES

    def first_link(a):
        pairs = [(2 * e + c, 2 * (e ^ (1 + c)) + c) for e in range(ep) for c in range(2)]
        return lax.ppermute(a, ("ep", "tp"), pairs)

    def second_link(a):
        pairs = [(2 * e + c, 2 * (e ^ (2 - c)) + c) for e in range(ep) for c in range(2)]
        return lax.ppermute(a, ("ep", "tp"), pairs)

    def shift(a, steps):
        return lax.ppermute(a, "ep", [(e, (e + QUAD * steps) % ep) for e in range(ep)])

    def other_core(a):
        return lax.ppermute(a, "tp", [(0, 1), (1, 0)])

    block = call(
        functools.partial(route_kernel, ep, capacity, aside),
        jax.ShapeDtypeStruct((half, width + aside), BF16),
        (tokens, copied, scores.T, expert_ids.T),
        spaces=[pl.ANY, pltpu.SMEM, VMEM, VMEM],
        scratch=[pltpu.SemaphoreType.DMA],
        limit=None,
    )

    def load(gate, up, down):
        return call(
            load_kernel,
            (
                jax.ShapeDtypeStruct((width, units), BF16),
                jax.ShapeDtypeStruct((width, units), BF16),
                jax.ShapeDtypeStruct((units, share), BF16),
                jax.ShapeDtypeStruct((units, share), BF16),
            ),
            (gate, up, down),
            spaces=[pl.ANY] * 3,
            scratch=[pltpu.SemaphoreType.DMA((4,))],
            limit=41 << 20,
        )

    def experts(pair, far, tpair, tfar):
        hidden, scale = call(
            functools.partial(hidden_kernel, ep),
            (
                jax.ShapeDtypeStruct((quad_rows, units), BF16),
                jax.ShapeDtypeStruct((quad_rows, LANES), F32),
            ),
            (pair, far, tpair, tfar, gate, up),
            flops=4 * quad_rows * width * units,
        )
        return hidden, scale, other_core(hidden)

    def finish(hidden, scale, other):
        return call(
            functools.partial(down_kernel, half),
            (
                jax.ShapeDtypeStruct((quad_rows // 2, share), F32),
                jax.ShapeDtypeStruct((quad_rows // 2, share), BF16),
            ),
            (hidden, other, scale, down_mine, down_received),
            flops=4 * quad_rows * share * units,
        )

    def join(a, b):
        return jnp.concatenate([a, b], axis=0)

    came = {0: block}
    near = {0: first_link(block)}
    came[1] = shift(block, 1)
    gate, up, down_mine, down_sent = load(*lax.optimization_barrier((w_gate, w_up, w_down, block))[:3])
    down_received = other_core(down_sent)
    pairs, fars, held, sums, gots, parts, passes = {}, {}, {}, {}, {}, {}, {}

    def add_up(p, *ties):
        part = (after(sums[p][0], *ties) + gots[p].astype(F32)).reshape(2, 2, half, share)
        passes[p] = part[:, 1].reshape(2 * half, share).astype(BF16)
        parts[p] = part[:, 0].reshape(2 * half, share), second_link(passes[p])

    def multiply(p, *ties):
        far = after(fars[p], *ties)
        held[p] = experts(pairs[p], far, other_core(pairs[p]), other_core(far))

    def down_of(p, *ties):
        sums[p] = finish(after(held[p][0], *ties), *held[p][1:])
        gots[p] = first_link(sums[p][1])

    for p in range(planes):
        ties = [down_mine] if p == 0 else [fars[p - 1]]
        ties += [came[p + 1]] if 1 <= p < planes - 1 else []
        ties += [held[p - 2][0]] if p >= 2 else []
        pairs[p] = join(after(came[p], *ties), near[p])
        fars[p] = second_link(pairs[p])
        if p == 0:
            came[1] = after(came[1], pairs[0])
        if p + 1 < planes:
            near[p + 1] = first_link(came[p + 1])
        if p + 2 < planes:
            came[p + 2] = shift(came[p + 1], 1)
        if p >= 1:
            multiply(p - 1, pairs[p])
    for p in range(1, planes):
        if p not in held:
            multiply(p, sums[p - 1][1])
        down_of(p, *([pairs[p + 2]] if p + 2 < planes else [pairs[planes - 1]] if p + 2 == planes else []))
        if p >= 2:
            add_up(p - 1)
    down_of(0, sums[planes - 1][1], passes[1])
    add_up(planes - 1, sums[0][1])
    add_up(0, passes[planes - 1])
    carried = None
    for p in range(1, planes):
        total = parts[p][0] + after(parts[p][1], passes[(p + 1) % planes]).astype(F32)
        passing = (total if carried is None else carried.astype(F32) + total).astype(BF16)
        carried = shift(passing, 1)
    total = carried.astype(F32) + parts[0][0] + parts[0][1].astype(F32)
    mine_rows, other_rows = total[:half], total[half:]
    first = jnp.where(core == 0, mine_rows, other_rows)
    second = jnp.where(core == 0, other_rows, mine_rows)
    return jnp.concatenate([first, second], axis=0).astype(BF16)


def solution(mesh):
    in_specs = (
        P(("grp", "ep"), None),
        P(("grp", "ep"), None),
        P(("grp", "ep"), None),
        P("grp"),
        P("ep", None, "tp"),
        P("ep", None, "tp"),
        P("ep", "tp", None),
    )
    out_specs = P(("grp", "ep"), "tp")
    return jax.shard_map(body, mesh=mesh, in_specs=in_specs, out_specs=out_specs, check_vma=False)
```

```python
import functools

import jax
import jax.numpy as jnp
from jax import lax
from jax.experimental import pallas as pl
from jax.experimental.pallas import tpu as pltpu
from jax.sharding import PartitionSpec as P

BF16 = jnp.bfloat16
F32 = jnp.float32
QUAD = 4
LANES = 128
VMEM = pltpu.VMEM


def route_kernel(experts, capacity, aside, tokens_ref, copied_ref, scores_ref, ids_ref, block_ref, sem):
    top, rows = scores_ref.shape
    half, width = rows // 2, tokens_ref.shape[1]
    core = lax.axis_index("tp")
    copy = pltpu.make_async_copy(
        tokens_ref.at[pl.ds(pl.multiple_of(core * half, half), half), :], block_ref.at[:, :width], sem
    )
    copy.start()
    affinity = 1.0 / (1.0 + jnp.exp(-scores_ref[...]))
    gate = 2.5 * affinity / jnp.sum(affinity, axis=0, keepdims=True)
    ids = ids_ref[...]
    lane = lax.broadcasted_iota(jnp.int32, (aside, rows), 0)
    expert = jnp.where(lane < experts, lane, jnp.where(lane < 2 * experts, lane - experts, -1))
    member = jnp.zeros((aside, rows), F32)
    weight = jnp.zeros((aside, rows), F32)
    for k in range(top):
        here = ids[k : k + 1, :] == expert
        member = jnp.where(here, 1.0, member)
        weight = jnp.where(here, gate[k : k + 1, :], weight)
    copied = jnp.zeros((aside, 1), jnp.int32)
    for e in range(experts):
        copied = jnp.where(expert[:, :1] == e, copied_ref[e], copied)
    above = lax.broadcasted_iota(jnp.int32, (rows, rows), 0) < lax.broadcasted_iota(jnp.int32, (rows, rows), 1)
    rank = jnp.dot(member.astype(BF16), above.astype(F32).astype(BF16), preferred_element_type=F32)
    kept = (rank < capacity) | (copied == 1)
    weight = jnp.where(kept, weight, 0.0)
    high = weight.astype(BF16).astype(F32)
    beside = jnp.where(lane < experts, high, weight - high).T
    beside = jnp.where(core == 0, beside[:half], beside[half:])
    block_ref[:, width:] = beside.astype(BF16)
    copy.wait()


def load_kernel(gate_hbm, up_hbm, down_hbm, gate_ref, up_ref, mine_ref, sent_ref, sems):
    share = mine_ref.shape[1]
    core = lax.axis_index("tp")
    here = pl.multiple_of(core * share, LANES)
    there = pl.multiple_of((1 - core) * share, LANES)
    copies = [
        pltpu.make_async_copy(down_hbm.at[0, :, pl.ds(there, share)], sent_ref, sems.at[0]),
        pltpu.make_async_copy(gate_hbm.at[0], gate_ref, sems.at[1]),
        pltpu.make_async_copy(up_hbm.at[0], up_ref, sems.at[2]),
        pltpu.make_async_copy(down_hbm.at[0, :, pl.ds(here, share)], mine_ref, sems.at[3]),
    ]
    for c in copies:
        c.start()
    for c in copies:
        c.wait()


def hidden_kernel(experts, *refs):
    pieces, (gate_ref, up_ref, hidden_ref, scale_ref) = refs[:4], refs[4:]
    width, units = gate_ref.shape
    me = lax.axis_index("ep")
    n = pieces[0].shape[0]
    x = jnp.concatenate([p[:, :width] for p in pieces], axis=0)
    step = 256 if units % 256 == 0 else units
    for at in range(0, units, step):
        gate = jnp.dot(x, gate_ref[:, at : at + step], preferred_element_type=F32)
        up = jnp.dot(x, up_ref[:, at : at + step], preferred_element_type=F32)
        hidden_ref[:, at : at + step] = (gate / (1.0 + jnp.exp(-gate)) * up).astype(BF16)
    for i, p in enumerate(pieces):
        beside = p[:, width:].astype(F32)
        lane = lax.broadcasted_iota(jnp.int32, beside.shape, 1)
        mine = (lane == me) | (lane == me + experts)
        total = jnp.sum(jnp.where(mine, beside, 0.0), axis=1, keepdims=True)
        scale_ref[i * n : (i + 1) * n, :] = jnp.broadcast_to(total, (n, LANES))


def down_kernel(half, hidden_ref, other_ref, scale_ref, mine_ref, received_ref, kept_ref, sent_ref):
    n = hidden_ref.shape[0] // 2
    share = mine_ref.shape[1]
    hidden = hidden_ref[...]
    other = jnp.concatenate([other_ref[n:, :], other_ref[:n, :]], axis=0)
    scale = scale_ref[:, :1]
    step = 256 if share % 256 == 0 else share
    for at in range(0, share, step):
        y = jnp.dot(hidden, mine_ref[:, at : at + step], preferred_element_type=F32)
        y = y + jnp.dot(other, received_ref[:, at : at + step], preferred_element_type=F32)
        y = y * scale
        for ref, order in ((kept_ref, (0, 2, 4, 5)), (sent_ref, (1, 3, 6, 7))):
            for i, j in enumerate(order):
                ref[i * half : (i + 1) * half, at : at + step] = y[j * half : (j + 1) * half].astype(ref.dtype)


def call(kernel, outs, args, spaces=None, scratch=(), flops=0, limit=32 << 20):
    spaces = spaces or [VMEM] * len(args)
    return pl.pallas_call(
        kernel,
        out_shape=outs,
        in_specs=[pl.BlockSpec(memory_space=s) for s in spaces],
        out_specs=jax.tree.map(lambda _: pl.BlockSpec(memory_space=VMEM), outs),
        scratch_shapes=scratch,
        compiler_params=pltpu.CompilerParams(vmem_limit_bytes=limit),
        cost_estimate=pl.CostEstimate(flops=flops, bytes_accessed=sum(a.size * a.dtype.itemsize for a in args), transcendentals=0),
    )(*args)


def after(a, *deps):
    return lax.optimization_barrier((a,) + deps)[0]


def body(tokens, scores, expert_ids, copied, w_gate, w_up, w_down):
    ep = lax.axis_size("ep")
    core = lax.axis_index("tp")
    rows, width = tokens.shape
    top = expert_ids.shape[1]
    units = w_gate.shape[2]
    planes = ep // QUAD
    half = rows // 2
    share = width // 2
    quad_rows = QUAD * rows
    capacity = min(rows * top // ep, rows // 2)
    aside = -(-2 * ep // LANES) * LANES

    def first_link(a):
        pairs = [(2 * e + c, 2 * (e ^ (1 + c)) + c) for e in range(ep) for c in range(2)]
        return lax.ppermute(a, ("ep", "tp"), pairs)

    def second_link(a):
        pairs = [(2 * e + c, 2 * (e ^ (2 - c)) + c) for e in range(ep) for c in range(2)]
        return lax.ppermute(a, ("ep", "tp"), pairs)

    def shift(a, steps):
        return lax.ppermute(a, "ep", [(e, (e + QUAD * steps) % ep) for e in range(ep)])

    def other_core(a):
        return lax.ppermute(a, "tp", [(0, 1), (1, 0)])

    block = call(
        functools.partial(route_kernel, ep, capacity, aside),
        jax.ShapeDtypeStruct((half, width + aside), BF16),
        (tokens, copied, scores.T, expert_ids.T),
        spaces=[pl.ANY, pltpu.SMEM, VMEM, VMEM],
        scratch=[pltpu.SemaphoreType.DMA],
        limit=None,
    )

    def load(gate, up, down):
        return call(
            load_kernel,
            (
                jax.ShapeDtypeStruct((width, units), BF16),
                jax.ShapeDtypeStruct((width, units), BF16),
                jax.ShapeDtypeStruct((units, share), BF16),
                jax.ShapeDtypeStruct((units, share), BF16),
            ),
            (gate, up, down),
            spaces=[pl.ANY] * 3,
            scratch=[pltpu.SemaphoreType.DMA((4,))],
            limit=41 << 20,
        )

    def experts(pair, far, tpair, tfar):
        hidden, scale = call(
            functools.partial(hidden_kernel, ep),
            (
                jax.ShapeDtypeStruct((quad_rows, units), BF16),
                jax.ShapeDtypeStruct((quad_rows, LANES), F32),
            ),
            (pair, far, tpair, tfar, gate, up),
            flops=4 * quad_rows * width * units,
        )
        return hidden, scale, other_core(hidden)

    def finish(hidden, scale, other):
        return call(
            functools.partial(down_kernel, half),
            (
                jax.ShapeDtypeStruct((quad_rows // 2, share), F32),
                jax.ShapeDtypeStruct((quad_rows // 2, share), BF16),
            ),
            (hidden, other, scale, down_mine, down_received),
            flops=4 * quad_rows * share * units,
        )

    def join(a, b):
        return jnp.concatenate([a, b], axis=0)

    came = {0: block}
    near = {0: first_link(block)}
    came[1] = shift(block, 1)
    gate, up, down_mine, down_sent = load(*lax.optimization_barrier((w_gate, w_up, w_down, block))[:3])
    down_received = other_core(down_sent)
    pairs, fars, held, sums, gots, parts, passes = {}, {}, {}, {}, {}, {}, {}

    def add_up(p, *ties):
        part = (after(sums[p][0], *ties) + gots[p].astype(F32)).reshape(2, 2, half, share)
        passes[p] = part[:, 1].reshape(2 * half, share).astype(BF16)
        parts[p] = part[:, 0].reshape(2 * half, share), second_link(passes[p])

    def multiply(p, *ties):
        far = after(fars[p], *ties)
        held[p] = experts(pairs[p], far, other_core(pairs[p]), other_core(far))

    def down_of(p, *ties):
        sums[p] = finish(after(held[p][0], *ties), *held[p][1:])
        gots[p] = first_link(sums[p][1])

    for p in range(planes):
        ties = [down_mine] if p == 0 else [fars[p - 1]]
        ties += [came[p + 1]] if 1 <= p < planes - 1 else []
        ties += [held[p - 2][0]] if p >= 2 else []
        pairs[p] = join(after(came[p], *ties), near[p])
        fars[p] = shift(fars[2], 1) if p == 3 else second_link(pairs[p])
        if p == 0:
            came[1] = after(came[1], pairs[0])
        if p + 1 < planes:
            near[p + 1] = first_link(came[p + 1])
        if p + 2 < planes:
            came[p + 2] = shift(came[p + 1], 1)
        if p >= 1:
            multiply(p - 1, pairs[p])
    for p in range(1, planes):
        if p not in held:
            multiply(p, sums[p - 1][1])
        down_of(p, *([pairs[p + 2]] if p + 2 < planes else [pairs[planes - 1]] if p + 2 == planes else []))
        if p >= 2:
            add_up(p - 1)
    down_of(0, sums[planes - 1][1], passes[1])
    add_up(planes - 1, sums[0][1])
    add_up(0, passes[planes - 1])
    carried = None
    for p in range(1, planes):
        total = parts[p][0] + after(parts[p][1], *([passes[p + 1]] if p + 1 < planes else [])).astype(F32)
        passing = (total if carried is None else carried.astype(F32) + total).astype(BF16)
        carried = shift(passing, 1)
    total = carried.astype(F32) + parts[0][0] + parts[0][1].astype(F32)
    mine_rows, other_rows = total[:half], total[half:]
    first = jnp.where(core == 0, mine_rows, other_rows)
    second = jnp.where(core == 0, other_rows, mine_rows)
    return jnp.concatenate([first, second], axis=0).astype(BF16)


def solution(mesh):
    in_specs = (
        P(("grp", "ep"), None),
        P(("grp", "ep"), None),
        P(("grp", "ep"), None),
        P("grp"),
        P("ep", None, "tp"),
        P("ep", None, "tp"),
        P("ep", "tp", None),
    )
    out_specs = P(("grp", "ep"), "tp")
    return jax.shard_map(body, mesh=mesh, in_specs=in_specs, out_specs=out_specs, check_vma=False)
```
